32 devices in a mesh: group: 1, adapter: 16 (over z, y, core), mp: 2 (over x).
Axes of the slice: x: 2, y: 2, z: 4, core: 2. Of those that a mesh axis runs over, the one named last changes fastest.
Arguments:
- rows: bfloat16 [512, 8192], P(('group', 'adapter'), 'mp'), may hold values from -6 to 6
- request_adapter_index: int32 [512, 1], P(('group', 'adapter')), may hold values from 0 to 15; in each aligned block of 32 rows (0 to 31, 32 to 63, ...) at most 2 rows name the same one
- base_up_matrix: bfloat16 [8192, 14336], P('mp', 'adapter'), may hold values from -0.0625 to 0.0625
- adapter_down_weight: bfloat16 [16, 8192, 64], P('adapter', 'mp'), may hold values from -0.0625 to 0.0625
- adapter_up_weight: bfloat16 [16, 64, 14336], P(None, 'mp', 'adapter'), may hold values from -0.75 to 0.75
Outputs:
- projected: bfloat16 [512, 14336], P(('group', 'mp'), 'adapter')
The draws below stay inside these ranges and needn't reach their ends.
Inputs may be any that keep to these rules, and one draw needn't show every extreme that they name: `request_adapter_index`: in each aligned block of 32 rows (the rows of one index of adapter) no adapter is named by more than 2 rows, a bound that some block reaches; every adapter is named by some row.
All inputs are finite; a program needn't handle non-finite values.
Results may differ from the reference program's by a relative error of at most 0.0041.
Values may be sent and summed in bfloat16 or wider, within the bound.
A program may use at most 64 MiB of HBM per device.

```python
import math
import jax
import jax.numpy as jnp
import numpy as np
from jax import lax

MODEL_WIDTH = 8192
HIDDEN_UNITS = 14336
ADAPTER_RANK = 64
CAP = 2
ROW_DEV = 32
ROWS = 512
ADAPTER_TOTAL = 16


def shard_levels(stream_key, dims, pieces, smallest, largest):
    gain, own = 1.0, jax.random.fold_in(stream_key, 6)
    for position, shards_of in pieces:
        steps = jnp.exp(jax.random.uniform(jax.random.fold_in(own, position), (shards_of,), jnp.float32, smallest / len(pieces), largest / len(pieces)))
        gain = gain * jnp.repeat(steps, dims[position] // shards_of).reshape([-1 if axis == position else 1 for axis in range(len(dims))])
    return gain


def shared_out(key, own, number, rows, number_of, top, reach, skew):
    order = jax.random.permutation(key, number_of)
    heavy_load, ordinary = shares(number_of, rows * top, reach, skew, True), shares(number_of, rows * top, reach, skew, False)
    places = jnp.arange(number_of)

    def named(sizes, rotation):
        used = int((sizes > 0).sum())
        fixed = max(1, used // 4)
        passed = fixed + (places - fixed + rotation * (used - fixed)) % max(1, number_of - fixed)
        return jnp.zeros((number_of,), jnp.int32).at[order[jnp.where(places < fixed, places, passed)]].set(jnp.asarray(sizes, jnp.int32))

    sizes = jnp.where(number % 4 == 0, named(heavy_load, number // 4), named(ordinary, number - number // 4 - 1))
    mixed = jax.random.permutation(jax.random.fold_in(own, 3), number_of)
    donor, sink = mixed[0:number_of // 2 * 2:2], mixed[1:number_of // 2 * 2:2]
    room = jnp.minimum(sizes[donor] - 1, reach - sizes[sink]) // 2
    room = jnp.where((donor == order[0]) | (sink == order[0]) | (sizes[sink] == 0), 0, jnp.maximum(room, 0))
    passed = jax.random.randint(jax.random.fold_in(own, 4), (number_of // 2,), 0, 1 << 20) % (room + 1)
    sizes = sizes.at[donor].add(-passed).at[sink].add(passed)
    items = jnp.searchsorted(jnp.cumsum(sizes), jnp.arange(rows * top), side="right").astype(jnp.int32)
    table = items.reshape(top, rows).T
    table = table[jax.random.permutation(jax.random.fold_in(own, 1), rows)]
    rotation = jax.random.randint(jax.random.fold_in(own, 2), (rows, 1), 0, top)
    return jnp.take_along_axis(table, (jnp.arange(top)[None, :] + rotation) % top, axis=1)


def shares(amount, total, bound, slope, full):
    weights = [(1 << 20) // math.isqrt(standing ** slope) + 1 for standing in range(1, amount + 1)]
    largest = bound if full else min(bound, max(-(-total // amount), total * weights[0] // sum(weights)))
    least = 1 if total - largest >= amount - 1 else 0
    counts, surplus = [largest] + [least] * (amount - 1), total - largest - least * (amount - 1)
    while surplus > 0:
        candidates = [i for i in range(1, amount) if counts[i] < largest] or [i for i in range(1, amount) if counts[i] < bound]
        mass, budget = sum([weights[i] for i in candidates]), surplus
        for i in candidates:
            more = min(bound - counts[i], max(1, budget * weights[i] // mass), surplus)
            counts[i] = counts[i] + more
            surplus = surplus - more
    return np.array(counts)


def bell_draw(key, extent, width, bound, split=(), dtype=jnp.bfloat16):
    factor_of = shard_levels(key, extent, split, -0.22, 0.18) if split else 1.0
    entries = jax.random.normal(key, extent, jnp.float32) * width * factor_of
    return jnp.minimum(jnp.maximum(entries, -bound), bound).astype(dtype)


def setup_inputs(seed: int = 0, part: int = 0) -> dict:
    keys = jax.random.split(jax.random.key(seed), 6)
    part_splits = jax.random.split(jax.random.fold_in(keys[5], part), 6)
    rows = bell_draw(part_splits[0], (ROWS, MODEL_WIDTH), 1.0, 6.0, ((0, 16), (1, 2)))
    request_adapter_index_keys = jax.random.split(jax.random.fold_in(part_splits[1], 1), ROWS // ROW_DEV)
    request_adapter_index_turns = jax.random.permutation(jax.random.fold_in(part_splits[1], 3), ROWS // ROW_DEV)
    request_adapter_index = jax.vmap(lambda own, number: shared_out(jax.random.fold_in(part_splits[1], 2), own, number, ROW_DEV, ADAPTER_TOTAL, 1, CAP, 2))(request_adapter_index_keys, request_adapter_index_turns).reshape((ROWS, 1))
    base_up_matrix = bell_draw(keys[2], (MODEL_WIDTH, HIDDEN_UNITS), MODEL_WIDTH ** -0.5, 0.0625, ((0, 2), (1, 16)))
    adapter_down_weight = bell_draw(keys[3], (ADAPTER_TOTAL, MODEL_WIDTH, ADAPTER_RANK), MODEL_WIDTH ** -0.5, 0.0625, ((0, 16), (1, 2)))
    adapter_up_weight = bell_draw(keys[4], (ADAPTER_TOTAL, ADAPTER_RANK, HIDDEN_UNITS), ADAPTER_RANK ** -0.5, 0.75, ((1, 2), (2, 16)))
    return dict(rows=rows, request_adapter_index=request_adapter_index, base_up_matrix=base_up_matrix, adapter_down_weight=adapter_down_weight, adapter_up_weight=adapter_up_weight)


def reference(rows, request_adapter_index, base_up_matrix, adapter_down_weight, adapter_up_weight):
    ids = request_adapter_index[:, 0].astype(jnp.int32)

    def shrink_row(item):
        single_request, chosen_adapter = item
        return jnp.dot(single_request[None, :], adapter_down_weight[chosen_adapter], preferred_element_type=jnp.float32)[0]

    low = lax.map(shrink_row, (rows, ids)).astype(jnp.bfloat16)

    def expand_row(item):
        single_request, chosen_adapter = item
        return jnp.dot(single_request[None, :], adapter_up_weight[chosen_adapter], preferred_element_type=jnp.float32)[0]

    delta = lax.map(expand_row, (low, ids))
    base = jnp.dot(rows, base_up_matrix, preferred_element_type=jnp.float32)
    return (base + delta).astype(jnp.bfloat16)
```

```python
import functools

import jax
import jax.numpy as jnp
from jax import lax
from jax.experimental import pallas as pl
from jax.experimental.pallas import tpu as pltpu
from jax.sharding import PartitionSpec as P

CAP = 2
MESH = pl.DeviceIdType.MESH
F32 = jnp.float32
BF16 = jnp.bfloat16


def iota(shape, dim):
    return lax.broadcasted_iota(jnp.int32, shape, dim)


def kernel(
    dims, rows, ids, base, down, up, out,
    xg, w, dw, uw, acc, plow, slots, slot_row, part, part_in, low_own, low_all, sbuf, rbuf,
    lsem, ring_s, ring_r, sib_s, sib_r, slot_s, slot_r, part_s, part_r, low_s, low_r, out_s, out_r,
):
    owners, parts, folded = dims
    chips = owners // 2
    far = chips // 2
    home, features = rows.shape
    half = home // 2
    width = base.shape[1]
    rank = down.shape[1]
    rank_portion = up.shape[0] // owners
    total = owners * home
    mine = CAP * owners
    share = total // parts
    chunk = 128

    me = lax.axis_index("adapter")
    m = lax.axis_index("mp")
    core = lax.rem(me, 2)
    chip = me // 2
    if folded:
        y, z = lax.rem(chip, 2), chip // 2
        place = z + y * (chips - 1 - 2 * z)
    else:
        place = chip

    def device_at(q, c):
        q = lax.rem(q + 2 * chips, chips)
        if folded:
            y = q // (chips // 2)
            q = 2 * (q + y * (chips - 1 - 2 * q)) + y
        return 2 * q + c

    sibling = me + 1 - 2 * core
    ahead = (device_at(place + 1, core), device_at(place - 1, core))

    def peer(d):
        return lax.rem(me + d, owners)

    loads = [
        pltpu.make_async_copy(rows, xg.at[pl.ds(0, home)], lsem.at[0]),
        pltpu.make_async_copy(base, w, lsem.at[1]),
        pltpu.make_async_copy(down, dw, lsem.at[2]),
        pltpu.make_async_copy(up, uw, lsem.at[3]),
    ]
    for copy in loads:
        copy.start()

    barrier = pltpu.get_barrier_semaphore()

    def greet(d, _):
        pl.semaphore_signal(barrier, inc=1, device_id={"adapter": peer(d)}, device_id_type=MESH)
        return 0

    lax.fori_loop(1, owners, greet, 0)
    for d in range(1, parts):
        pl.semaphore_signal(barrier, inc=1, device_id={"mp": lax.rem(m + d, parts)}, device_id_type=MESH)

    lane = iota((home, 128), 1)
    row = iota((home, 128), 0)
    column = jnp.broadcast_to(ids[...], (home, 128)).astype(F32)
    inner = lax.rem(lane, home)
    across = jnp.sum(jnp.where(inner == row, column, 0.0), axis=0, keepdims=True)
    before = jnp.where((column == across) & (row < inner), 1.0, 0.0)
    position = jnp.sum(before, axis=0, keepdims=True)
    slot = across * mine + position + (CAP * me + 1).astype(F32)
    group_of = 128 // home
    here = iota((1, 128), 1) // home == lax.rem(me, group_of)
    slots[me] = jnp.broadcast_to(jnp.where(here, slot, 0.0), (8, 128))

    pl.semaphore_wait(barrier, owners - 1 + parts - 1)

    def reach(d, h):
        return far if d == h else far - 1

    def at(k, d, s, h):
        if k == 0:
            start = 0
        else:
            start = 2 * home + (k - 1) * 4 * home + (d * 2 * home if k < far else 0)
        return pl.ds(start + s * home + h * half, half)

    def ring(k, d, h):
        src = rows.at[pl.ds(h * half, half)] if k == 1 else xg.at[at(k - 1, d, 0, h)]
        return pltpu.make_async_remote_copy(
            src_ref=src, dst_ref=xg.at[at(k, d, 0, h)],
            send_sem=ring_s.at[d, k, h], recv_sem=ring_r.at[d, k, h],
            device_id={"adapter": ahead[d]}, device_id_type=MESH,
        )

    def across_chip(k, d, h):
        src = rows.at[pl.ds(h * half, half)] if k == 0 else xg.at[at(k, d, 0, h)]
        return pltpu.make_async_remote_copy(
            src_ref=src, dst_ref=xg.at[at(k, d, 1, h)],
            send_sem=sib_s.at[d, k, h], recv_sem=sib_r.at[d, k, h],
            device_id={"adapter": sibling}, device_id_type=MESH,
        )

    def slot_copy(d):
        return pltpu.make_async_remote_copy(
            src_ref=slots.at[me], dst_ref=slots.at[me],
            send_sem=slot_s.at[d], recv_sem=slot_r.at[d],
            device_id={"adapter": peer(d)}, device_id_type=MESH,
        )

    def low_copy(d):
        return pltpu.make_async_remote_copy(
            src_ref=low_own, dst_ref=low_all.at[pl.ds(pl.multiple_of(me * mine, mine), mine)],
            send_sem=low_s.at[d], recv_sem=low_r.at[d],
            device_id={"adapter": peer(d)}, device_id_type=MESH,
        )

    def each_peer(action):
        def go(d, _):
            action(d)
            return 0

        lax.fori_loop(1, owners, go, 0)

    for h in range(2):
        for d in range(2):
            ring(1, d, h).start()
    for h in range(2):
        across_chip(0, 0, h).start()
    each_peer(lambda d: slot_copy(d).start())

    def region(k):
        count = 2 * home if k in (0, far) else 4 * home
        start = 0 if k == 0 else 2 * home + (k - 1) * 4 * home
        origins = []
        for d in range(count // (2 * home)):
            q = place - k if d == 0 else place + k
            origins += [device_at(q, core), device_at(q, 1 - core)]
        return start, count, [pl.multiple_of(o * home, home) for o in origins]

    def low_part(k):
        start, count, origins = region(k)
        r = jnp.dot(xg[start:start + count, :], dw[...], preferred_element_type=F32)
        for i, o in enumerate(origins):
            plow[pl.ds(o, home), :] = r[i * home:(i + 1) * home]

    def base_part(k):
        start, count, origins = region(k)
        for n in range(0, width, 256):
            e = min(n + 256, width)
            r = jnp.dot(xg[start:start + count, :], w[:, n:e], preferred_element_type=F32)
            for i, o in enumerate(origins):
                acc[pl.ds(o, home), n:e] = r[i * home:(i + 1) * home]

    def siblings_in(k):
        for h in range(2):
            for d in range(2):
                if (k == 0 and d == 0) or (k > 0 and k <= reach(d, h)):
                    across_chip(k, d, h).wait_recv()

    for k in range(1, far + 1):
        for h in range(2):
            for d in range(2):
                if k <= reach(d, h):
                    ring(k, d, h).wait_recv()
                    if k + 1 <= reach(d, h):
                        ring(k + 1, d, h).start()
                    across_chip(k, d, h).start()
        if k == 1:
            for copy in loads[:3]:
                copy.wait()
        siblings_in(k - 1)
        low_part(k - 1)
        base_part(k - 1)
    siblings_in(far)
    low_part(far)

    each_peer(lambda d: slot_copy(d).wait_recv())
    for q in range(total // 128):
        line = slots[q * group_of]
        for i in range(1, group_of):
            line = line + slots[q * group_of + i]
        slot_row[:, q * 128:(q + 1) * 128] = line
    wanted = (iota((mine, total), 0) + (me * mine + 1)).astype(F32)
    pick = jnp.where(wanted == slot_row[0:1, :], 1.0, 0.0)
    part[...] = jnp.dot(pick, plow[...], preferred_element_type=F32, precision=lax.Precision.HIGHEST)

    def part_copy(d):
        return pltpu.make_async_remote_copy(
            src_ref=part, dst_ref=part_in.at[d - 1],
            send_sem=part_s.at[d], recv_sem=part_r.at[d],
            device_id={"mp": lax.rem(m + d, parts)}, device_id_type=MESH,
        )

    for d in range(1, parts):
        part_copy(d).start()
    base_part(far)
    low = part[...]
    for d in range(1, parts):
        part_copy(d).wait_recv()
        low = low + part_in[d - 1]
    low_own[...] = jnp.broadcast_to(me.astype(F32), (mine, 128)).astype(BF16)
    low_own[:, :rank] = low.astype(BF16)
    each_peer(lambda d: low_copy(d).start())
    low_all[pl.ds(pl.multiple_of(me * mine, mine), mine), :] = low_own[...]
    spread = jnp.where(
        iota((128, owners * rank_portion), 0)
        == m * rank_portion + lax.rem(iota((128, owners * rank_portion), 1), rank_portion),
        1.0, 0.0,
    ).astype(BF16)
    of_column = (iota((chunk, owners * rank_portion), 1) // rank_portion).astype(F32)
    loads[3].wait()
    each_peer(lambda d: low_copy(d).wait_recv())

    def finished(first):
        all_slots = (iota((owners * mine, chunk), 0) + 1).astype(F32)
        hit = jnp.where(all_slots == slot_row[0:1, pl.ds(first, chunk)], 1.0, 0.0).astype(BF16)
        low_rows = lax.dot_general(
            hit, low_all[...], (((0,), (0,)), ((), ())), preferred_element_type=F32
        )
        copies = jnp.dot(low_rows.astype(BF16), spread, preferred_element_type=F32)
        wide = jnp.where(of_column == low_rows[:, rank:rank + 1], copies, 0.0).astype(BF16)
        return acc[pl.ds(first, chunk), :] + jnp.dot(wide, uw[...], preferred_element_type=F32)

    def out_copy(d, c):
        return pltpu.make_async_remote_copy(
            src_ref=sbuf.at[d - 1, c], dst_ref=rbuf.at[d - 1, c],
            send_sem=out_s.at[d, c], recv_sem=out_r.at[d, c],
            device_id={"mp": lax.rem(m + d, parts)}, device_id_type=MESH,
        )

    pieces = share // chunk
    for d in range(1, parts):
        to = lax.rem(m + d, parts)
        for c in range(pieces):
            sbuf[d - 1, c] = finished(pl.multiple_of(to * share + c * chunk, chunk)).astype(BF16)
            out_copy(d, c).start()
    for c in range(pieces):
        first = pl.multiple_of(m * share + c * chunk, chunk)
        acc[pl.ds(first, chunk), :] = finished(first)
    for c in range(pieces):
        value = acc[pl.ds(pl.multiple_of(m * share + c * chunk, chunk), chunk), :]
        for d in range(1, parts):
            out_copy(d, c).wait_recv()
            value = value + rbuf[d - 1, c].astype(F32)
        out[c * chunk:(c + 1) * chunk, :] = value.astype(BF16)

    for h in range(2):
        for d in range(2):
            for k in range(1, reach(d, h) + 1):
                ring(k, d, h).wait_send()
                across_chip(k, d, h).wait_send()
        across_chip(0, 0, h).wait_send()
    each_peer(lambda d: slot_copy(d).wait_send())
    each_peer(lambda d: low_copy(d).wait_send())
    for d in range(1, parts):
        part_copy(d).wait_send()
        for c in range(pieces):
            out_copy(d, c).wait_send()


def solution(mesh):
    owners, parts = mesh.shape["adapter"], mesh.shape["mp"]
    folded = mesh.shape["group"] == 1

    def body(rows, request_adapter_index, base_up_matrix, adapter_down_weight, adapter_up_weight):
        home, features = rows.shape
        width = base_up_matrix.shape[1]
        rank = adapter_down_weight.shape[2]
        rank_portion = adapter_up_weight.shape[1]
        total = owners * home
        mine = CAP * owners
        share = total // parts
        pieces = share // 128
        far = owners // 4
        any_space = pl.BlockSpec(memory_space=pl.ANY)
        in_vmem = pl.BlockSpec(memory_space=pltpu.VMEM)
        dma = pltpu.SemaphoreType.DMA
        flops = 2 * total * features * (width + rank)
        return pl.pallas_call(
            functools.partial(kernel, (owners, parts, folded)),
            out_shape=jax.ShapeDtypeStruct((share, width), BF16),
            in_specs=[any_space, in_vmem, any_space, any_space, any_space],
            out_specs=in_vmem,
            scratch_shapes=[
                pltpu.VMEM((total, features), BF16),
                pltpu.VMEM((features, width), BF16),
                pltpu.VMEM((features, rank), BF16),
                pltpu.VMEM((owners * rank_portion, width), BF16),
                pltpu.VMEM((total, width), F32),
                pltpu.VMEM((total, rank), F32),
                pltpu.VMEM((owners, 8, 128), F32),
                pltpu.VMEM((8, total), F32),
                pltpu.VMEM((mine, rank), F32),
                pltpu.VMEM((parts - 1, mine, rank), F32),
                pltpu.VMEM((mine, 128), BF16),
                pltpu.VMEM((owners * mine, 128), BF16),
                pltpu.VMEM((parts - 1, pieces, 128, width), BF16),
                pltpu.VMEM((parts - 1, pieces, 128, width), BF16),
                dma((4,)),
                dma((2, far + 1, 2)),
                dma((2, far + 1, 2)),
                dma((2, far + 1, 2)),
                dma((2, far + 1, 2)),
                dma((owners,)),
                dma((owners,)),
                dma((parts,)),
                dma((parts,)),
                dma((owners,)),
                dma((owners,)),
                dma((parts, pieces)),
                dma((parts, pieces)),
            ],
            compiler_params=pltpu.CompilerParams(
                collective_id=0, has_side_effects=True, vmem_limit_bytes=56 * 1024 * 1024
            ),
            cost_estimate=pl.CostEstimate(
                flops=flops, bytes_accessed=2 * features * width, transcendentals=0
            ),
        )(
            rows,
            request_adapter_index,
            base_up_matrix,
            adapter_down_weight.reshape(features, rank),
            adapter_up_weight.reshape(owners * rank_portion, width),
        )

    return jax.shard_map(
        body,
        mesh=mesh,
        in_specs=(
            P(("group", "adapter"), "mp"),
            P(("group", "adapter"), None),
            P("mp", "adapter"),
            P("adapter", "mp", None),
            P(None, "mp", "adapter"),
        ),
        out_specs=P(("group", "mp"), "adapter"),
        check_vma=False,
    )
```

```python
import functools

import jax
import jax.numpy as jnp
from jax import lax
from jax.experimental import pallas as pl
from jax.experimental.pallas import tpu as pltpu
from jax.sharding import PartitionSpec as P

CAP = 2
MESH = pl.DeviceIdType.MESH
F32 = jnp.float32
BF16 = jnp.bfloat16


def iota(shape, dim):
    return lax.broadcasted_iota(jnp.int32, shape, dim)


def kernel(
    dims, rows, ids, base, down, up, out,
    xg, w, dw, uw, acc, plow, slots, slot_row, part, part_in, low_own, low_all, sbuf, rbuf,
    lsem, ring_s, ring_r, sib_s, sib_r, slot_s, slot_r, part_s, part_r, low_s, low_r, out_s, out_r, up_s, up_r,
):
    owners, parts, folded = dims
    chips = owners // 2
    far = chips // 2
    home, features = rows.shape
    half = home // 2
    width = base.shape[1]
    rank = down.shape[0]
    rank_portion = up.shape[0] // owners
    total = owners * home
    mine = CAP * owners
    share = total // parts
    chunk = 128
    some = mine // parts
    part_chips = chips // parts

    me = lax.axis_index("adapter")
    m = lax.axis_index("mp")
    core = lax.rem(me, 2)
    chip = me // 2
    if folded:
        y, z = lax.rem(chip, 2), chip // 2
        place = z + y * (chips - 1 - 2 * z)
    else:
        place = chip

    def device_at(q, c):
        q = lax.rem(q + 2 * chips, chips)
        if folded:
            y = q // (chips // 2)
            q = 2 * (q + y * (chips - 1 - 2 * q)) + y
        return 2 * q + c

    sibling = me + 1 - 2 * core
    ahead = (device_at(place + 1, core), device_at(place - 1, core))

    def peer(d):
        return lax.rem(me + d, owners)

    loads = [
        pltpu.make_async_copy(rows, xg.at[pl.ds(0, home)], lsem.at[0]),
        pltpu.make_async_copy(base, w, lsem.at[1]),
        pltpu.make_async_copy(down, dw, lsem.at[2]),
        pltpu.make_async_copy(up, uw.at[0], lsem.at[3]),
    ]
    for copy in loads:
        copy.start()

    barrier = pltpu.get_barrier_semaphore()

    def greet(d, _):
        pl.semaphore_signal(barrier, inc=1, device_id={"adapter": peer(d)}, device_id_type=MESH)
        return 0

    lax.fori_loop(1, owners, greet, 0)
    for d in range(1, parts):
        pl.semaphore_signal(barrier, inc=1, device_id={"mp": lax.rem(m + d, parts)}, device_id_type=MESH)

    lane = iota((home, 128), 1)
    row = iota((home, 128), 0)
    square = jnp.broadcast_to(ids[...].astype(F32), (home, home))
    diagonal = iota((home, home), 0) == iota((home, home), 1)
    column = jnp.sum(jnp.where(diagonal, square, 0.0), axis=1, keepdims=True)
    column = jnp.broadcast_to(column, (home, 128))
    inner = lax.rem(lane, home)
    across = jnp.sum(jnp.where(inner == row, column, 0.0), axis=0, keepdims=True)
    before = jnp.where((column == across) & (row < inner), 1.0, 0.0)
    position = jnp.sum(before, axis=0, keepdims=True)
    slot = across * mine + position + (CAP * me + 1).astype(F32)
    group_of = 128 // home
    here = iota((1, 128), 1) // home == lax.rem(me, group_of)
    slots[me] = jnp.broadcast_to(jnp.where(here, slot, 0.0), (8, 128))

    pl.semaphore_wait(barrier, owners - 1 + parts - 1)

    def reach(d, h):
        return far if d == h else far - 1

    def at(k, d, s, h):
        if k == 0:
            start = 0
        else:
            start = 2 * home + (k - 1) * 4 * home + (d * 2 * home if k < far else 0)
        return pl.ds(start + s * home + h * half, half)

    def ring(k, d, h):
        src = rows.at[pl.ds(h * half, half)] if k == 1 else xg.at[at(k - 1, d, 0, h)]
        return pltpu.make_async_remote_copy(
            src_ref=src, dst_ref=xg.at[at(k, d, 0, h)],
            send_sem=ring_s.at[d, k, h], recv_sem=ring_r.at[d, k, h],
            device_id={"adapter": ahead[d]}, device_id_type=MESH,
        )

    def across_chip(k, d, h):
        src = rows.at[pl.ds(h * half, half)] if k == 0 else xg.at[at(k, d, 0, h)]
        return pltpu.make_async_remote_copy(
            src_ref=src, dst_ref=xg.at[at(k, d, 1, h)],
            send_sem=sib_s.at[d, k, h], recv_sem=sib_r.at[d, k, h],
            device_id={"adapter": sibling}, device_id_type=MESH,
        )

    def slot_copy(d):
        return pltpu.make_async_remote_copy(
            src_ref=slots.at[me], dst_ref=slots.at[me],
            send_sem=slot_s.at[d], recv_sem=slot_r.at[d],
            device_id={"adapter": peer(d)}, device_id_type=MESH,
        )

    def low_copy(d):
        return pltpu.make_async_remote_copy(
            src_ref=low_own, dst_ref=low_all.at[pl.ds(pl.multiple_of(me * some, some), some)],
            send_sem=low_s.at[d], recv_sem=low_r.at[d],
            device_id={"adapter": peer(d)}, device_id_type=MESH,
        )

    def each_peer(action):
        def go(d, _):
            action(d)
            return 0

        lax.fori_loop(1, owners, go, 0)

    for h in range(2):
        for d in range(2):
            ring(1, d, h).start()
    for h in range(2):
        across_chip(0, 0, h).start()
    each_peer(lambda d: slot_copy(d).start())

    def up_copy(d):
        return pltpu.make_async_remote_copy(
            src_ref=up, dst_ref=uw.at[d],
            send_sem=up_s.at[d], recv_sem=up_r.at[d],
            device_id={"mp": lax.rem(m + d, parts)}, device_id_type=MESH,
        )

    for d in range(1, parts):
        up_copy(d).start()

    def out_copy(c, to, d):
        local = pl.ds(pl.multiple_of(lax.rem(c, part_chips) * 2 * home, 2 * home), 2 * home)
        return pltpu.make_async_remote_copy(
            src_ref=sbuf.at[c], dst_ref=rbuf.at[d - 1, local],
            send_sem=out_s.at[c], recv_sem=out_r.at[d - 1, lax.rem(c, part_chips)],
            device_id={"mp": to}, device_id_type=MESH,
        )

    def send_part(c):
        to = c // part_chips

        @pl.when(to != m)
        def _():
            rows_of = pl.ds(pl.multiple_of(c * 2 * home, 2 * home), 2 * home)
            sbuf[c] = acc[rows_of, :].astype(BF16)
            out_copy(c, to, lax.rem(to - m + parts, parts)).start()

    def region(k):
        count = 2 * home if k in (0, far) else 4 * home
        start = 0 if k == 0 else 2 * home + (k - 1) * 4 * home
        origins = []
        for d in range(count // (2 * home)):
            q = place - k if d == 0 else place + k
            origins += [device_at(q, core), device_at(q, 1 - core)]
        return start, count, [pl.multiple_of(o * home, home) for o in origins]

    def low_part(k):
        start, count, origins = region(k)
        r = lax.dot_general(
            xg[start:start + count, :], dw[...], (((1,), (1,)), ((), ())),
            preferred_element_type=F32,
        )
        for i, o in enumerate(origins):
            plow[pl.ds(o, home), :] = r[i * home:(i + 1) * home]

    def base_part(k):
        start, count, origins = region(k)
        for n in range(0, width, 256):
            e = min(n + 256, width)
            r = jnp.dot(xg[start:start + count, :], w[:, n:e], preferred_element_type=F32)
            for i, o in enumerate(origins):
                acc[pl.ds(o, home), n:e] = r[i * home:(i + 1) * home]
        for o in origins[::2]:
            send_part(o // (2 * home))

    def siblings_in(k):
        for h in range(2):
            for d in range(2):
                if (k == 0 and d == 0) or (k > 0 and k <= reach(d, h)):
                    across_chip(k, d, h).wait_recv()

    for k in range(1, far + 1):
        for h in range(2):
            for d in range(2):
                if k <= reach(d, h):
                    ring(k, d, h).wait_recv()
                    if k + 1 <= reach(d, h):
                        ring(k + 1, d, h).start()
                    across_chip(k, d, h).start()
        if k == 1:
            for copy in loads[:3]:
                copy.wait()
        siblings_in(k - 1)
        low_part(k - 1)
        base_part(k - 1)
    siblings_in(far)
    low_part(far)

    each_peer(lambda d: slot_copy(d).wait_recv())
    for q in range(total // 128):
        line = slots[q * group_of]
        for i in range(1, group_of):
            line = line + slots[q * group_of + i]
        slot_row[:, q * 128:(q + 1) * 128] = line
    wanted = (iota((mine, total), 0) + (me * mine + 1)).astype(F32)
    pick = jnp.where(wanted == slot_row[0:1, :], 1.0, 0.0)
    part[...] = jnp.dot(pick, plow[...], preferred_element_type=F32, precision=lax.Precision.HIGHEST)

    def own_part(q):
        return pl.ds(pl.multiple_of(q * some, some), some)

    def part_copy(d):
        to = lax.rem(m + d, parts)
        return pltpu.make_async_remote_copy(
            src_ref=part.at[own_part(to)], dst_ref=part_in.at[d - 1],
            send_sem=part_s.at[d], recv_sem=part_r.at[d],
            device_id={"mp": to}, device_id_type=MESH,
        )

    for d in range(1, parts):
        part_copy(d).start()
    base_part(far)
    low = part[own_part(m), :]
    for d in range(1, parts):
        part_copy(d).wait_recv()
        low = low + part_in[d - 1]
    low_own[...] = jnp.broadcast_to(me.astype(F32), (some, 128)).astype(BF16)
    low_own[:, :rank] = low.astype(BF16)
    each_peer(lambda d: low_copy(d).start())
    low_all[own_part(me), :] = low_own[...]
    wide_shape = (128, owners * rank_portion)
    within = lax.rem(iota(wide_shape, 1), rank_portion)
    of_column = (iota((chunk, owners * rank_portion), 1) // rank_portion).astype(F32)
    ordinal = iota((owners * some, chunk), 0)
    all_slots = (ordinal // some * mine + m * some + lax.rem(ordinal, some) + 1).astype(F32)
    loads[3].wait()
    for d in range(1, parts):
        up_copy(d).wait_recv()
    each_peer(lambda d: low_copy(d).wait_recv())

    pieces = share // chunk
    for c in range(pieces):
        first = pl.multiple_of(m * share + c * chunk, chunk)
        hit = jnp.where(all_slots == slot_row[0:1, pl.ds(first, chunk)], 1.0, 0.0).astype(BF16)
        low_rows = lax.dot_general(
            hit, low_all[...], (((0,), (0,)), ((), ())), preferred_element_type=F32
        )
        value = acc[pl.ds(first, chunk), :]
        for d in range(parts):
            ranks = lax.rem(m - d + parts, parts) * rank_portion
            spread = jnp.where(iota(wide_shape, 0) == ranks + within, 1.0, 0.0).astype(BF16)
            copies = jnp.dot(low_rows.astype(BF16), spread, preferred_element_type=F32)
            wide = jnp.where(of_column == low_rows[:, rank:rank + 1], copies, 0.0).astype(BF16)
            value = value + jnp.dot(wide, uw[d], preferred_element_type=F32)
        acc[pl.ds(first, chunk), :] = value
    for c in range(pieces):
        value = acc[pl.ds(pl.multiple_of(m * share + c * chunk, chunk), chunk), :]
        for d in range(1, parts):
            for i in range(c * chunk // (2 * home), (c + 1) * chunk // (2 * home)):
                out_copy(i, lax.rem(m + d, parts), d).wait_recv()
            value = value + rbuf[d - 1, c * chunk:(c + 1) * chunk, :].astype(F32)
        out[c * chunk:(c + 1) * chunk, :] = value.astype(BF16)

    for h in range(2):
        for d in range(2):
            for k in range(1, reach(d, h) + 1):
                ring(k, d, h).wait_send()
                across_chip(k, d, h).wait_send()
        across_chip(0, 0, h).wait_send()
    each_peer(lambda d: slot_copy(d).wait_send())
    each_peer(lambda d: low_copy(d).wait_send())
    for d in range(1, parts):
        part_copy(d).wait_send()
        up_copy(d).wait_send()
        to = lax.rem(m + d, parts)
        for i in range(part_chips):
            out_copy(to * part_chips + i, to, d).wait_send()


def solution(mesh):
    owners, parts = mesh.shape["adapter"], mesh.shape["mp"]
    folded = mesh.shape["group"] == 1

    def body(rows, request_adapter_index, base_up_matrix, adapter_down_weight, adapter_up_weight):
        home, features = rows.shape
        width = base_up_matrix.shape[1]
        rank = adapter_down_weight.shape[2]
        rank_portion = adapter_up_weight.shape[1]
        total = owners * home
        mine = CAP * owners
        share = total // parts
        some = mine // parts
        chips = owners // 2
        far = owners // 4
        any_space = pl.BlockSpec(memory_space=pl.ANY)
        in_vmem = pl.BlockSpec(memory_space=pltpu.VMEM)
        dma = pltpu.SemaphoreType.DMA
        flops = 2 * total * features * (width + rank)
        return pl.pallas_call(
            functools.partial(kernel, (owners, parts, folded)),
            out_shape=jax.ShapeDtypeStruct((share, width), BF16),
            in_specs=[any_space, in_vmem, any_space, any_space, any_space],
            out_specs=in_vmem,
            scratch_shapes=[
                pltpu.VMEM((total, features), BF16),
                pltpu.VMEM((features, width), BF16),
                pltpu.VMEM((rank, features), BF16),
                pltpu.VMEM((parts, owners * rank_portion, width), BF16),
                pltpu.VMEM((total, width), F32),
                pltpu.VMEM((total, rank), F32),
                pltpu.VMEM((owners, 8, 128), F32),
                pltpu.VMEM((8, total), F32),
                pltpu.VMEM((mine, rank), F32),
                pltpu.VMEM((parts - 1, some, rank), F32),
                pltpu.VMEM((some, 128), BF16),
                pltpu.VMEM((owners * some, 128), BF16),
                pltpu.VMEM((chips, 2 * home, width), BF16),
                pltpu.VMEM((parts - 1, share, width), BF16),
                dma((4,)),
                dma((2, far + 1, 2)),
                dma((2, far + 1, 2)),
                dma((2, far + 1, 2)),
                dma((2, far + 1, 2)),
                dma((owners,)),
                dma((owners,)),
                dma((parts,)),
                dma((parts,)),
                dma((owners,)),
                dma((owners,)),
                dma((chips,)),
                dma((parts - 1, chips // parts)),
                dma((parts,)),
                dma((parts,)),
            ],
            compiler_params=pltpu.CompilerParams(
                collective_id=0, has_side_effects=True, vmem_limit_bytes=56 * 1024 * 1024
            ),
            cost_estimate=pl.CostEstimate(
                flops=flops, bytes_accessed=2 * features * width, transcendentals=0
            ),
        )(
            rows,
            request_adapter_index.reshape(1, home),
            base_up_matrix,
            jnp.swapaxes(adapter_down_weight, 1, 2).reshape(rank, features),
            adapter_up_weight.reshape(owners * rank_portion, width),
        )

    return jax.shard_map(
        body,
        mesh=mesh,
        in_specs=(
            P(("group", "adapter"), "mp"),
            P(("group", "adapter"), None),
            P("mp", "adapter"),
            P("adapter", "mp", None),
            P(None, "mp", "adapter"),
        ),
        out_specs=P(("group", "mp"), "adapter"),
        check_vma=False,
    )
```

```python
import functools

import jax
import jax.numpy as jnp
from jax import lax
from jax.experimental import pallas as pl
from jax.experimental.pallas import tpu as pltpu
from jax.sharding import PartitionSpec as P

CAP = 2
MESH = pl.DeviceIdType.MESH
F32 = jnp.float32
BF16 = jnp.bfloat16


def iota(shape, dim):
    return lax.broadcasted_iota(jnp.int32, shape, dim)


def kernel(
    dims, rows, ids, base, down, up, out,
    xg, w, dw, uw, acc, plow, slots, slot_row, part, part_in, low_own, low_all, sbuf, rbuf,
    lsem, ring_s, ring_r, sib_s, sib_r, slot_s, slot_r, part_s, part_r, low_s, low_r, out_s, out_r, up_s, up_r,
):
    owners, parts, folded = dims
    chips = owners // 2
    far = chips // 2
    home, features = rows.shape
    half = home // 2
    width = base.shape[1]
    rank = down.shape[0]
    rank_portion = up.shape[0] // owners
    total = owners * home
    mine = CAP * owners
    share = total // parts
    chunk = 128
    some = mine // parts
    part_chips = chips // parts

    me = lax.axis_index("adapter")
    m = lax.axis_index("mp")
    core = lax.rem(me, 2)
    chip = me // 2
    if folded:
        y, z = lax.rem(chip, 2), chip // 2
        place = z + y * (chips - 1 - 2 * z)
    else:
        place = chip

    def device_at(q, c):
        q = lax.rem(q + 2 * chips, chips)
        if folded:
            y = q // (chips // 2)
            q = 2 * (q + y * (chips - 1 - 2 * q)) + y
        return 2 * q + c

    sibling = me + 1 - 2 * core
    ahead = (device_at(place + 1, core), device_at(place - 1, core))

    def peer(d):
        return lax.rem(me + d, owners)

    loads = [
        pltpu.make_async_copy(rows, xg.at[pl.ds(0, home)], lsem.at[0]),
        pltpu.make_async_copy(base, w, lsem.at[1]),
        pltpu.make_async_copy(down, dw, lsem.at[2]),
        pltpu.make_async_copy(up, uw.at[0], lsem.at[3]),
    ]
    for copy in loads:
        copy.start()

    barrier = pltpu.get_barrier_semaphore()

    def greet(d, _):
        pl.semaphore_signal(barrier, inc=1, device_id={"adapter": peer(d)}, device_id_type=MESH)
        return 0

    lax.fori_loop(1, owners, greet, 0)
    for d in range(1, parts):
        pl.semaphore_signal(barrier, inc=1, device_id={"mp": lax.rem(m + d, parts)}, device_id_type=MESH)

    lane = iota((home, 128), 1)
    row = iota((home, 128), 0)
    square = jnp.broadcast_to(ids[...].astype(F32), (home, home))
    diagonal = iota((home, home), 0) == iota((home, home), 1)
    column = jnp.sum(jnp.where(diagonal, square, 0.0), axis=1, keepdims=True)
    column = jnp.broadcast_to(column, (home, 128))
    inner = lax.rem(lane, home)
    across = jnp.sum(jnp.where(inner == row, column, 0.0), axis=0, keepdims=True)
    before = jnp.where((column == across) & (row < inner), 1.0, 0.0)
    position = jnp.sum(before, axis=0, keepdims=True)
    slot = across * mine + position + (CAP * me + 1).astype(F32)
    group_of = 128 // home
    here = iota((1, 128), 1) // home == lax.rem(me, group_of)
    slots[me] = jnp.broadcast_to(jnp.where(here, slot, 0.0), (8, 128))

    pl.semaphore_wait(barrier, owners - 1 + parts - 1)

    def reach(d, h):
        return far if d == h else far - 1

    def at(k, d, s, h):
        if k == 0:
            start = 0
        else:
            start = 2 * home + (k - 1) * 4 * home + (d * 2 * home if k < far else 0)
        return pl.ds(start + s * home + h * half, half)

    def ring(k, d, h):
        src = rows.at[pl.ds(h * half, half)] if k == 1 else xg.at[at(k - 1, d, 0, h)]
        return pltpu.make_async_remote_copy(
            src_ref=src, dst_ref=xg.at[at(k, d, 0, h)],
            send_sem=ring_s.at[d, k, h], recv_sem=ring_r.at[d, k, h],
            device_id={"adapter": ahead[d]}, device_id_type=MESH,
        )

    def across_chip(k, d, h):
        src = rows.at[pl.ds(h * half, half)] if k == 0 else xg.at[at(k, d, 0, h)]
        return pltpu.make_async_remote_copy(
            src_ref=src, dst_ref=xg.at[at(k, d, 1, h)],
            send_sem=sib_s.at[d, k, h], recv_sem=sib_r.at[d, k, h],
            device_id={"adapter": sibling}, device_id_type=MESH,
        )

    def slot_copy(d):
        return pltpu.make_async_remote_copy(
            src_ref=slots.at[me], dst_ref=slots.at[me],
            send_sem=slot_s.at[d], recv_sem=slot_r.at[d],
            device_id={"adapter": peer(d)}, device_id_type=MESH,
        )

    def low_copy(d):
        return pltpu.make_async_remote_copy(
            src_ref=low_own, dst_ref=low_all.at[pl.ds(pl.multiple_of(me * some, some), some)],
            send_sem=low_s.at[d], recv_sem=low_r.at[d],
            device_id={"adapter": peer(d)}, device_id_type=MESH,
        )

    def each_peer(action):
        def go(d, _):
            action(d)
            return 0

        lax.fori_loop(1, owners, go, 0)

    for h in range(2):
        for d in range(2):
            ring(1, d, h).start()
    for h in range(2):
        across_chip(0, 0, h).start()
    each_peer(lambda d: slot_copy(d).start())

    def up_copy(d):
        return pltpu.make_async_remote_copy(
            src_ref=up, dst_ref=uw.at[d],
            send_sem=up_s.at[d], recv_sem=up_r.at[d],
            device_id={"mp": lax.rem(m + d, parts)}, device_id_type=MESH,
        )

    for d in range(1, parts):
        up_copy(d).start()

    def out_copy(c, to, d):
        local = pl.ds(pl.multiple_of(lax.rem(c, part_chips) * 2 * home, 2 * home), 2 * home)
        return pltpu.make_async_remote_copy(
            src_ref=sbuf.at[c], dst_ref=rbuf.at[d - 1, local],
            send_sem=out_s.at[c], recv_sem=out_r.at[d - 1, lax.rem(c, part_chips)],
            device_id={"mp": to}, device_id_type=MESH,
        )

    def send_part(c):
        to = c // part_chips

        @pl.when(to != m)
        def _():
            rows_of = pl.ds(pl.multiple_of(c * 2 * home, 2 * home), 2 * home)
            sbuf[c] = acc[rows_of, :].astype(BF16)
            out_copy(c, to, lax.rem(to - m + parts, parts)).start()

    def region(k):
        count = 2 * home if k in (0, far) else 4 * home
        start = 0 if k == 0 else 2 * home + (k - 1) * 4 * home
        origins = []
        for d in range(count // (2 * home)):
            q = place - k if d == 0 else place + k
            origins += [device_at(q, core), device_at(q, 1 - core)]
        return start, count, [pl.multiple_of(o * home, home) for o in origins]

    def low_part(k):
        start, count, origins = region(k)
        r = lax.dot_general(
            xg[start:start + count, :], dw[...], (((1,), (1,)), ((), ())),
            preferred_element_type=F32,
        )
        for i, o in enumerate(origins):
            plow[pl.ds(o, home), :] = r[i * home:(i + 1) * home]

    def base_part(k):
        start, count, origins = region(k)
        for n in range(0, width, 256):
            e = min(n + 256, width)
            r = jnp.dot(xg[start:start + count, :], w[:, n:e], preferred_element_type=F32)
            for i, o in enumerate(origins):
                acc[pl.ds(o, home), n:e] = r[i * home:(i + 1) * home]
        for o in origins[::2]:
            send_part(o // (2 * home))

    def siblings_in(k):
        for h in range(2):
            for d in range(2):
                if (k == 0 and d == 0) or (k > 0 and k <= reach(d, h)):
                    across_chip(k, d, h).wait_recv()

    def arrivals(k, h):
        for d in range(2):
            if k <= reach(d, h):
                ring(k, d, h).wait_recv()
                if k + 1 <= reach(d, h):
                    ring(k + 1, d, h).start()
                across_chip(k, d, h).start()

    def products(k):
        siblings_in(k)
        low_part(k)
        base_part(k)

    for copy in loads[:3]:
        copy.wait()
    for k in range(1, far):
        arrivals(k, 0)
        products(k - 1)
        arrivals(k, 1)
    products(far - 1)

    each_peer(lambda d: slot_copy(d).wait_recv())
    for q in range(total // 128):
        line = slots[q * group_of]
        for i in range(1, group_of):
            line = line + slots[q * group_of + i]
        slot_row[:, q * 128:(q + 1) * 128] = line
    wanted = (iota((mine, total), 0) + (me * mine + 1)).astype(F32)
    pick = jnp.where(wanted == slot_row[0:1, :], 1.0, 0.0)
    for h in range(2):
        arrivals(far, h)
    siblings_in(far)
    low_part(far)
    part[...] = jnp.dot(pick, plow[...], preferred_element_type=F32, precision=lax.Precision.HIGHEST)

    def own_part(q):
        return pl.ds(pl.multiple_of(q * some, some), some)

    def part_copy(d):
        to = lax.rem(m + d, parts)
        return pltpu.make_async_remote_copy(
            src_ref=part.at[own_part(to)], dst_ref=part_in.at[d - 1],
            send_sem=part_s.at[d], recv_sem=part_r.at[d],
            device_id={"mp": to}, device_id_type=MESH,
        )

    for d in range(1, parts):
        part_copy(d).start()
    base_part(far)
    low = part[own_part(m), :]
    for d in range(1, parts):
        part_copy(d).wait_recv()
        low = low + part_in[d - 1]
    low_own[...] = jnp.broadcast_to(me.astype(F32), (some, 128)).astype(BF16)
    low_own[:, :rank] = low.astype(BF16)
    each_peer(lambda d: low_copy(d).start())
    low_all[own_part(me), :] = low_own[...]
    wide_shape = (128, owners * rank_portion)
    within = lax.rem(iota(wide_shape, 1), rank_portion)
    of_column = (iota((chunk, owners * rank_portion), 1) // rank_portion).astype(F32)
    ordinal = iota((owners * some, chunk), 0)
    all_slots = (ordinal // some * mine + m * some + lax.rem(ordinal, some) + 1).astype(F32)
    loads[3].wait()
    for d in range(1, parts):
        up_copy(d).wait_recv()
    pieces = share // chunk
    spreads = []
    for d in range(parts):
        ranks = lax.rem(m - d + parts, parts) * rank_portion
        spreads.append(jnp.where(iota(wide_shape, 0) == ranks + within, 1.0, 0.0).astype(BF16))
    hits = []
    for c in range(pieces):
        first = pl.multiple_of(m * share + c * chunk, chunk)
        line = slot_row[0:1, pl.ds(first, chunk)]
        hits.append(jnp.where(all_slots == line, 1.0, 0.0).astype(BF16))
    each_peer(lambda d: low_copy(d).wait_recv())

    for c in range(pieces):
        first = pl.multiple_of(m * share + c * chunk, chunk)
        low_rows = lax.dot_general(
            hits[c], low_all[...], (((0,), (0,)), ((), ())), preferred_element_type=F32
        )
        value = acc[pl.ds(first, chunk), :]
        for d in range(parts):
            copies = jnp.dot(low_rows.astype(BF16), spreads[d], preferred_element_type=F32)
            wide = jnp.where(of_column == low_rows[:, rank:rank + 1], copies, 0.0).astype(BF16)
            value = value + jnp.dot(wide, uw[d], preferred_element_type=F32)
        acc[pl.ds(first, chunk), :] = value
    for c in range(pieces):
        value = acc[pl.ds(pl.multiple_of(m * share + c * chunk, chunk), chunk), :]
        for d in range(1, parts):
            for i in range(c * chunk // (2 * home), (c + 1) * chunk // (2 * home)):
                out_copy(i, lax.rem(m + d, parts), d).wait_recv()
            value = value + rbuf[d - 1, c * chunk:(c + 1) * chunk, :].astype(F32)
        out[c * chunk:(c + 1) * chunk, :] = value.astype(BF16)

    for h in range(2):
        for d in range(2):
            for k in range(1, reach(d, h) + 1):
                ring(k, d, h).wait_send()
                across_chip(k, d, h).wait_send()
        across_chip(0, 0, h).wait_send()
    each_peer(lambda d: slot_copy(d).wait_send())
    each_peer(lambda d: low_copy(d).wait_send())
    for d in range(1, parts):
        part_copy(d).wait_send()
        up_copy(d).wait_send()
        to = lax.rem(m + d, parts)
        for i in range(part_chips):
            out_copy(to * part_chips + i, to, d).wait_send()


def solution(mesh):
    owners, parts = mesh.shape["adapter"], mesh.shape["mp"]
    folded = mesh.shape["group"] == 1

    def body(rows, request_adapter_index, base_up_matrix, adapter_down_weight, adapter_up_weight):
        home, features = rows.shape
        width = base_up_matrix.shape[1]
        rank = adapter_down_weight.shape[2]
        rank_portion = adapter_up_weight.shape[1]
        total = owners * home
        mine = CAP * owners
        share = total // parts
        some = mine // parts
        chips = owners // 2
        far = owners // 4
        any_space = pl.BlockSpec(memory_space=pl.ANY)
        in_vmem = pl.BlockSpec(memory_space=pltpu.VMEM)
        dma = pltpu.SemaphoreType.DMA
        flops = 2 * total * features * (width + rank)
        return pl.pallas_call(
            functools.partial(kernel, (owners, parts, folded)),
            out_shape=jax.ShapeDtypeStruct((share, width), BF16),
            in_specs=[any_space, in_vmem, any_space, any_space, any_space],
            out_specs=in_vmem,
            scratch_shapes=[
                pltpu.VMEM((total, features), BF16),
                pltpu.VMEM((features, width), BF16),
                pltpu.VMEM((rank, features), BF16),
                pltpu.VMEM((parts, owners * rank_portion, width), BF16),
                pltpu.VMEM((total, width), F32),
                pltpu.VMEM((total, rank), F32),
                pltpu.VMEM((owners, 8, 128), F32),
                pltpu.VMEM((8, total), F32),
                pltpu.VMEM((mine, rank), F32),
                pltpu.VMEM((parts - 1, some, rank), F32),
                pltpu.VMEM((some, 128), BF16),
                pltpu.VMEM((owners * some, 128), BF16),
                pltpu.VMEM((chips, 2 * home, width), BF16),
                pltpu.VMEM((parts - 1, share, width), BF16),
                dma((4,)),
                dma((2, far + 1, 2)),
                dma((2, far + 1, 2)),
                dma((2, far + 1, 2)),
                dma((2, far + 1, 2)),
                dma((owners,)),
                dma((owners,)),
                dma((parts,)),
                dma((parts,)),
                dma((owners,)),
                dma((owners,)),
                dma((chips,)),
                dma((parts - 1, chips // parts)),
                dma((parts,)),
                dma((parts,)),
            ],
            compiler_params=pltpu.CompilerParams(
                collective_id=0, has_side_effects=True, vmem_limit_bytes=56 * 1024 * 1024
            ),
            cost_estimate=pl.CostEstimate(
                flops=flops, bytes_accessed=2 * features * width, transcendentals=0
            ),
        )(
            rows,
            request_adapter_index.reshape(1, home),
            base_up_matrix,
            jnp.swapaxes(adapter_down_weight, 1, 2).reshape(rank, features),
            adapter_up_weight.reshape(owners * rank_portion, width),
        )

    return jax.shard_map(
        body,
        mesh=mesh,
        in_specs=(
            P(("group", "adapter"), "mp"),
            P(("group", "adapter"), None),
            P("mp", "adapter"),
            P("adapter", "mp", None),
            P(None, "mp", "adapter"),
        ),
        out_specs=P(("group", "mp"), "adapter"),
        check_vma=False,
    )
```

```python
import functools

import jax
import jax.numpy as jnp
from jax import lax
from jax.experimental import pallas as pl
from jax.experimental.pallas import tpu as pltpu
from jax.sharding import PartitionSpec as P

CAP = 2
MESH = pl.DeviceIdType.MESH
F32 = jnp.float32
BF16 = jnp.bfloat16


def iota(shape, dim):
    return lax.broadcasted_iota(jnp.int32, shape, dim)


def kernel(
    dims, rows, ids, base, down, up, out,
    xg, w, dw, uw, acc, plow, slots, slot_row, part, part_in, low_own, low_all, sbuf, rbuf,
    lsem, ring_s, ring_r, sib_s, sib_r, slot_s, slot_r, part_s, part_r, low_s, low_r, out_s, out_r, up_s, up_r,
):
    owners, parts, folded = dims
    chips = owners // 2
    far = chips // 2
    home, features = rows.shape
    half = home // 2
    width = base.shape[1]
    rank = down.shape[0]
    rank_portion = up.shape[0] // owners
    total = owners * home
    mine = CAP * owners
    share = total // parts
    chunk = 128
    some = mine // parts
    part_chips = chips // parts

    me = lax.axis_index("adapter")
    m = lax.axis_index("mp")
    core = lax.rem(me, 2)
    chip = me // 2
    if folded:
        y, z = lax.rem(chip, 2), chip // 2
        place = z + y * (chips - 1 - 2 * z)
    else:
        place = chip

    def device_at(q, c):
        q = lax.rem(q + 2 * chips, chips)
        if folded:
            y = q // (chips // 2)
            q = 2 * (q + y * (chips - 1 - 2 * q)) + y
        return 2 * q + c

    sibling = me + 1 - 2 * core
    ahead = (device_at(place + 1, core), device_at(place - 1, core))

    def peer(d):
        return lax.rem(me + d, owners)

    loads = [
        pltpu.make_async_copy(rows, xg.at[pl.ds(0, home)], lsem.at[0]),
        pltpu.make_async_copy(base, w, lsem.at[1]),
        pltpu.make_async_copy(down, dw, lsem.at[2]),
        pltpu.make_async_copy(up, uw.at[0], lsem.at[3]),
    ]
    for copy in loads:
        copy.start()

    barrier = pltpu.get_barrier_semaphore()

    def greet(d, _):
        pl.semaphore_signal(barrier, inc=1, device_id={"adapter": peer(d)}, device_id_type=MESH)
        return 0

    lax.fori_loop(1, owners, greet, 0)
    for d in range(1, parts):
        pl.semaphore_signal(barrier, inc=1, device_id={"mp": lax.rem(m + d, parts)}, device_id_type=MESH)

    lane = iota((home, 128), 1)
    row = iota((home, 128), 0)
    square = jnp.broadcast_to(ids[...].astype(F32), (home, home))
    diagonal = iota((home, home), 0) == iota((home, home), 1)
    column = jnp.sum(jnp.where(diagonal, square, 0.0), axis=1, keepdims=True)
    column = jnp.broadcast_to(column, (home, 128))
    inner = lax.rem(lane, home)
    across = jnp.sum(jnp.where(inner == row, column, 0.0), axis=0, keepdims=True)
    before = jnp.where((column == across) & (row < inner), 1.0, 0.0)
    position = jnp.sum(before, axis=0, keepdims=True)
    slot = across * mine + position + (CAP * me + 1).astype(F32)
    group_of = 128 // home
    here = iota((1, 128), 1) // home == lax.rem(me, group_of)
    slots[me] = jnp.broadcast_to(jnp.where(here, slot, 0.0), (8, 128))

    pl.semaphore_wait(barrier, owners - 1 + parts - 1)

    def reach(d, h):
        return far if d == h else far - 1

    def at(k, d, s, h):
        if k == 0:
            start = 0
        else:
            start = 2 * home + (k - 1) * 4 * home + (d * 2 * home if k < far else 0)
        return pl.ds(start + s * home + h * half, half)

    def ring(k, d, h):
        src = rows.at[pl.ds(h * half, half)] if k == 1 else xg.at[at(k - 1, d, 0, h)]
        return pltpu.make_async_remote_copy(
            src_ref=src, dst_ref=xg.at[at(k, d, 0, h)],
            send_sem=ring_s.at[d, k, h], recv_sem=ring_r.at[d, k, h],
            device_id={"adapter": ahead[d]}, device_id_type=MESH,
        )

    def across_chip(k, d, h):
        src = rows.at[pl.ds(h * half, half)] if k == 0 else xg.at[at(k, d, 0, h)]
        return pltpu.make_async_remote_copy(
            src_ref=src, dst_ref=xg.at[at(k, d, 1, h)],
            send_sem=sib_s.at[d, k, h], recv_sem=sib_r.at[d, k, h],
            device_id={"adapter": sibling}, device_id_type=MESH,
        )

    def slot_copy(d):
        return pltpu.make_async_remote_copy(
            src_ref=slots.at[me], dst_ref=slots.at[me],
            send_sem=slot_s.at[d], recv_sem=slot_r.at[d],
            device_id={"adapter": peer(d)}, device_id_type=MESH,
        )

    def low_copy(d):
        return pltpu.make_async_remote_copy(
            src_ref=low_own, dst_ref=low_all.at[pl.ds(pl.multiple_of(me * some, some), some)],
            send_sem=low_s.at[d], recv_sem=low_r.at[d],
            device_id={"adapter": peer(d)}, device_id_type=MESH,
        )

    def each_peer(action):
        def go(d, _):
            action(d)
            return 0

        lax.fori_loop(1, owners, go, 0)

    for d in range(2):
        ring(1, d, 0).start()
    for h in range(2):
        across_chip(0, 0, h).start()
    each_peer(lambda d: slot_copy(d).start())

    def up_copy(d):
        return pltpu.make_async_remote_copy(
            src_ref=up, dst_ref=uw.at[d],
            send_sem=up_s.at[d], recv_sem=up_r.at[d],
            device_id={"mp": lax.rem(m + d, parts)}, device_id_type=MESH,
        )

    for d in range(1, parts):
        up_copy(d).start()

    def out_copy(c, to, d):
        local = pl.ds(pl.multiple_of(lax.rem(c, part_chips) * 2 * home, 2 * home), 2 * home)
        return pltpu.make_async_remote_copy(
            src_ref=sbuf.at[c], dst_ref=rbuf.at[d - 1, local],
            send_sem=out_s.at[c], recv_sem=out_r.at[d - 1, lax.rem(c, part_chips)],
            device_id={"mp": to}, device_id_type=MESH,
        )

    def send_part(c):
        to = c // part_chips

        @pl.when(to != m)
        def _():
            rows_of = pl.ds(pl.multiple_of(c * 2 * home, 2 * home), 2 * home)
            sbuf[c] = acc[rows_of, :].astype(BF16)
            out_copy(c, to, lax.rem(to - m + parts, parts)).start()

    def region(k):
        count = 2 * home if k in (0, far) else 4 * home
        start = 0 if k == 0 else 2 * home + (k - 1) * 4 * home
        origins = []
        for d in range(count // (2 * home)):
            q = place - k if d == 0 else place + k
            origins += [device_at(q, core), device_at(q, 1 - core)]
        return start, count, [pl.multiple_of(o * home, home) for o in origins]

    def low_part(k):
        start, count, origins = region(k)
        r = lax.dot_general(
            xg[start:start + count, :], dw[...], (((1,), (1,)), ((), ())),
            preferred_element_type=F32,
        )
        for i, o in enumerate(origins):
            plow[pl.ds(o, home), :] = r[i * home:(i + 1) * home]

    def base_part(k):
        start, count, origins = region(k)
        for n in range(0, width, 256):
            e = min(n + 256, width)
            r = jnp.dot(xg[start:start + count, :], w[:, n:e], preferred_element_type=F32)
            for i, o in enumerate(origins):
                acc[pl.ds(o, home), n:e] = r[i * home:(i + 1) * home]
        for o in origins[::2]:
            send_part(o // (2 * home))

    def siblings_in(k):
        for h in range(2):
            for d in range(2):
                if (k == 0 and d == 0) or (k > 0 and k <= reach(d, h)):
                    across_chip(k, d, h).wait_recv()

    def arrivals(k, h):
        for d in range(2):
            if k <= reach(d, h):
                ring(k, d, h).wait_recv()
                if k + 1 <= reach(d, h):
                    ring(k + 1, d, h).start()
                across_chip(k, d, h).start()

    def products(k):
        siblings_in(k)
        low_part(k)
        base_part(k)

    for d in range(2):
        ring(1, d, 0).wait_send()
        ring(1, d, 1).start()
    for copy in loads[:3]:
        copy.wait()
    for k in range(1, far):
        arrivals(k, 0)
        products(k - 1)
        arrivals(k, 1)
    products(far - 1)

    each_peer(lambda d: slot_copy(d).wait_recv())
    for q in range(total // 128):
        line = slots[q * group_of]
        for i in range(1, group_of):
            line = line + slots[q * group_of + i]
        slot_row[:, q * 128:(q + 1) * 128] = line
    wanted = (iota((mine, total), 0) + (me * mine + 1)).astype(F32)
    pick = jnp.where(wanted == slot_row[0:1, :], 1.0, 0.0)
    for h in range(2):
        arrivals(far, h)
    siblings_in(far)
    low_part(far)
    part[...] = jnp.dot(pick, plow[...], preferred_element_type=F32, precision=lax.Precision.HIGHEST)

    def own_part(q):
        return pl.ds(pl.multiple_of(q * some, some), some)

    def part_copy(d):
        to = lax.rem(m + d, parts)
        return pltpu.make_async_remote_copy(
            src_ref=part.at[own_part(to)], dst_ref=part_in.at[d - 1],
            send_sem=part_s.at[d], recv_sem=part_r.at[d],
            device_id={"mp": to}, device_id_type=MESH,
        )

    for d in range(1, parts):
        part_copy(d).start()
    base_part(far)
    low = part[own_part(m), :]
    for d in range(1, parts):
        part_copy(d).wait_recv()
        low = low + part_in[d - 1]
    low_own[...] = jnp.broadcast_to(me.astype(F32), (some, 128)).astype(BF16)
    low_own[:, :rank] = low.astype(BF16)
    each_peer(lambda d: low_copy(d).start())
    low_all[own_part(me), :] = low_own[...]
    wide_shape = (128, owners * rank_portion)
    within = lax.rem(iota(wide_shape, 1), rank_portion)
    of_column = (iota((chunk, owners * rank_portion), 1) // rank_portion).astype(F32)
    ordinal = iota((owners * some, chunk), 0)
    all_slots = (ordinal // some * mine + m * some + lax.rem(ordinal, some) + 1).astype(F32)
    loads[3].wait()
    for d in range(1, parts):
        up_copy(d).wait_recv()
    pieces = share // chunk
    spreads = []
    for d in range(parts):
        ranks = lax.rem(m - d + parts, parts) * rank_portion
        spreads.append(jnp.where(iota(wide_shape, 0) == ranks + within, 1.0, 0.0).astype(BF16))
    hits = []
    for c in range(pieces):
        first = pl.multiple_of(m * share + c * chunk, chunk)
        line = slot_row[0:1, pl.ds(first, chunk)]
        hits.append(jnp.where(all_slots == line, 1.0, 0.0).astype(BF16))
    each_peer(lambda d: low_copy(d).wait_recv())

    for c in range(pieces):
        first = pl.multiple_of(m * share + c * chunk, chunk)
        low_rows = lax.dot_general(
            hits[c], low_all[...], (((0,), (0,)), ((), ())), preferred_element_type=F32
        )
        value = acc[pl.ds(first, chunk), :]
        for d in range(parts):
            copies = jnp.dot(low_rows.astype(BF16), spreads[d], preferred_element_type=F32)
            wide = jnp.where(of_column == low_rows[:, rank:rank + 1], copies, 0.0).astype(BF16)
            value = value + jnp.dot(wide, uw[d], preferred_element_type=F32)
        acc[pl.ds(first, chunk), :] = value
    for c in range(pieces):
        value = acc[pl.ds(pl.multiple_of(m * share + c * chunk, chunk), chunk), :]
        for d in range(1, parts):
            for i in range(c * chunk // (2 * home), (c + 1) * chunk // (2 * home)):
                out_copy(i, lax.rem(m + d, parts), d).wait_recv()
            value = value + rbuf[d - 1, c * chunk:(c + 1) * chunk, :].astype(F32)
        out[c * chunk:(c + 1) * chunk, :] = value.astype(BF16)

    for h in range(2):
        for d in range(2):
            for k in range(1, reach(d, h) + 1):
                if k > 1 or h > 0:
                    ring(k, d, h).wait_send()
                across_chip(k, d, h).wait_send()
        across_chip(0, 0, h).wait_send()
    each_peer(lambda d: slot_copy(d).wait_send())
    each_peer(lambda d: low_copy(d).wait_send())
    for d in range(1, parts):
        part_copy(d).wait_send()
        up_copy(d).wait_send()
        to = lax.rem(m + d, parts)
        for i in range(part_chips):
            out_copy(to * part_chips + i, to, d).wait_send()


def solution(mesh):
    owners, parts = mesh.shape["adapter"], mesh.shape["mp"]
    folded = mesh.shape["group"] == 1

    def body(rows, request_adapter_index, base_up_matrix, adapter_down_weight, adapter_up_weight):
        home, features = rows.shape
        width = base_up_matrix.shape[1]
        rank = adapter_down_weight.shape[2]
        rank_portion = adapter_up_weight.shape[1]
        total = owners * home
        mine = CAP * owners
        share = total // parts
        some = mine // parts
        chips = owners // 2
        far = owners // 4
        any_space = pl.BlockSpec(memory_space=pl.ANY)
        in_vmem = pl.BlockSpec(memory_space=pltpu.VMEM)
        dma = pltpu.SemaphoreType.DMA
        flops = 2 * total * features * (width + rank)
        return pl.pallas_call(
            functools.partial(kernel, (owners, parts, folded)),
            out_shape=jax.ShapeDtypeStruct((share, width), BF16),
            in_specs=[any_space, in_vmem, any_space, any_space, any_space],
            out_specs=in_vmem,
            scratch_shapes=[
                pltpu.VMEM((total, features), BF16),
                pltpu.VMEM((features, width), BF16),
                pltpu.VMEM((rank, features), BF16),
                pltpu.VMEM((parts, owners * rank_portion, width), BF16),
                pltpu.VMEM((total, width), F32),
                pltpu.VMEM((total, rank), F32),
                pltpu.VMEM((owners, 8, 128), F32),
                pltpu.VMEM((8, total), F32),
                pltpu.VMEM((mine, rank), F32),
                pltpu.VMEM((parts - 1, some, rank), F32),
                pltpu.VMEM((some, 128), BF16),
                pltpu.VMEM((owners * some, 128), BF16),
                pltpu.VMEM((chips, 2 * home, width), BF16),
                pltpu.VMEM((parts - 1, share, width), BF16),
                dma((4,)),
                dma((2, far + 1, 2)),
                dma((2, far + 1, 2)),
                dma((2, far + 1, 2)),
                dma((2, far + 1, 2)),
                dma((owners,)),
                dma((owners,)),
                dma((parts,)),
                dma((parts,)),
                dma((owners,)),
                dma((owners,)),
                dma((chips,)),
                dma((parts - 1, chips // parts)),
                dma((parts,)),
                dma((parts,)),
            ],
            compiler_params=pltpu.CompilerParams(
                collective_id=0, has_side_effects=True, vmem_limit_bytes=56 * 1024 * 1024
            ),
            cost_estimate=pl.CostEstimate(
                flops=flops, bytes_accessed=2 * features * width, transcendentals=0
            ),
        )(
            rows,
            request_adapter_index.reshape(1, home),
            base_up_matrix,
            jnp.swapaxes(adapter_down_weight, 1, 2).reshape(rank, features),
            adapter_up_weight.reshape(owners * rank_portion, width),
        )

    return jax.shard_map(
        body,
        mesh=mesh,
        in_specs=(
            P(("group", "adapter"), "mp"),
            P(("group", "adapter"), None),
            P("mp", "adapter"),
            P("adapter", "mp", None),
            P(None, "mp", "adapter"),
        ),
        out_specs=P(("group", "mp"), "adapter"),
        check_vma=False,
    )
```
